32 devices in a mesh: groups: 2 (over y), ex: 4 (over z), ey: 4 (over x, core).
Axes of the slice: x: 2, y: 2, z: 4, core: 2. Of those that a mesh axis runs over, the one named last changes fastest.
Arguments:
- tokens: bfloat16 [128, 7168], P(('groups', 'ex', 'ey')), parts along dimension 0, may hold values from -6 to 6
- route: int32 [128, 2], P(('groups', 'ex', 'ey')), parts along dimension 0, may hold values from 0 to 3, all different within a row; in each aligned block of 4 rows (0 to 3, 4 to 7, ...) at most 4 rows name the same one
- gates: float32 [128, 2], P(('groups', 'ex', 'ey')), parts along dimension 0, may hold values from 0.2 to 1.5
- w_gate: bfloat16 [4, 7168, 2048], P('ex', None, 'ey'), may hold values from -0.0625 to 0.0625
- w_up: bfloat16 [4, 7168, 2048], P('ex', None, 'ey'), may hold values from -0.0625 to 0.0625
- w_down: bfloat16 [4, 2048, 7168], P('ex', 'ey'), may hold values from -0.125 to 0.125
Outputs:
- mixed: bfloat16 [128, 7168], P(('groups', 'ex', 'ey')), parts along dimension 0
The draws below stay inside these ranges and needn't reach their ends.
There are 2 independent parts, one for each index of `groups`. The reference program is written for one: setup_inputs(seed, part) draws one part's arguments, and reference() takes and returns one part's arrays. A program takes and returns all parts, laid end to end along the dimension named above; an argument that names none is the same for every part. Nothing has to cross between parts.
Inputs may be any that keep to these rules, and one draw needn't show every extreme that they name: `route`: each row names 2 different experts; within the 4 rows of one device no expert is named by more than 4 rows, and in some device's rows some expert is named by exactly 4 rows.
All inputs are finite; a program needn't handle non-finite values.
Results may differ from the reference program's by a relative error of at most 0.0066.
Values may be sent and summed in bfloat16 or wider, within the bound.
A program may use at most 128 MiB of HBM per device.

```python
import math
import jax
import jax.numpy as jnp
import numpy as np
from jax import lax

D = 7168
FF = 2048
TOK_DEV = 4
EXPERTS = 4
TOPK = 2
CAP = 4
TOKENS = 64
N_EX = 4
N_EY = 4


def shard_levels(rng, shape, shards, smallest, largest):
    gain = 1.0
    for axis_at, parts in shards:
        heights = jax.random.uniform(jax.random.fold_in(jax.random.fold_in(rng, 6), axis_at), (parts,), jnp.float32, smallest / len(shards), largest / len(shards))
        gain = gain * jnp.repeat(jnp.exp(heights), shape[axis_at] // parts).reshape((-1,) + (1,) * (len(shape) - 1 - axis_at))
    return gain


def routed_block(own_key, own, number, rows, amount, top, most, slope):
    order = jax.random.permutation(own_key, amount)
    heavy_load, usual = shares(amount, rows * top, most, slope, True), shares(amount, rows * top, most, slope, False)
    places = jnp.arange(amount)

    def named(lengths, rotation):
        used = int((lengths > 0).sum())
        fixed = max(1, used // 4)
        moved = fixed + (places - fixed + rotation * (used - fixed)) % max(1, amount - fixed)
        return jnp.zeros((amount,), jnp.int32).at[order[jnp.where(places < fixed, places, moved)]].set(jnp.asarray(lengths, jnp.int32))

    lengths = jnp.where(number % 4 == 0, named(heavy_load, number // 4), named(usual, number - number // 4 - 1))
    mixed = jax.random.permutation(jax.random.fold_in(own, 3), amount)
    giver, sink = mixed[0:amount // 2 * 2:2], mixed[1:amount // 2 * 2:2]
    room = jnp.minimum(lengths[giver] - 1, most - lengths[sink]) // 2
    room = jnp.where((giver == order[0]) | (sink == order[0]) | (lengths[sink] == 0), 0, jnp.maximum(room, 0))
    moved = jax.random.randint(jax.random.fold_in(own, 4), (amount // 2,), 0, 1 << 20) % (room + 1)
    lengths = lengths.at[giver].add(-moved).at[sink].add(moved)
    labels = jnp.searchsorted(jnp.cumsum(lengths), jnp.arange(rows * top), side="right").astype(jnp.int32)
    table = labels.reshape(top, rows).T
    table = table[jax.random.permutation(jax.random.fold_in(own, 1), rows)]
    rotation = jax.random.randint(jax.random.fold_in(own, 2), (rows, 1), 0, top)
    return jnp.take_along_axis(table, (jnp.arange(top)[None, :] + rotation) % top, axis=1)


def shares(number_of, total, most, lean, full):
    loads = [(1 << 20) // math.isqrt(grade ** lean) + 1 for grade in range(1, number_of + 1)]
    largest = most if full else min(most, max(-(-total // number_of), total * loads[0] // sum(loads)))
    least = 1 if total - largest >= number_of - 1 else 0
    counts, surplus = [largest] + [least] * (number_of - 1), total - largest - least * (number_of - 1)
    while surplus > 0:
        free = [i for i in range(1, number_of) if counts[i] < largest] or [i for i in range(1, number_of) if counts[i] < most]
        whole, left = sum([loads[i] for i in free]), surplus
        for i in free:
            addition = min(most - counts[i], max(1, left * loads[i] // whole), surplus)
            counts[i] = counts[i] + addition
            surplus = surplus - addition
    return np.array(counts)


def gaussian(key, extent, scale, most, cuts=(), kind=jnp.bfloat16):
    values = scale * jax.random.normal(key, extent, jnp.float32)
    if cuts:
        values = values * shard_levels(key, extent, cuts, -0.22, 0.18)
    return jnp.clip(values, -most, most).astype(kind)


def setup_inputs(seed: int = 0, part: int = 0) -> dict:
    keys = jax.random.split(jax.random.key(seed), 7)
    own_keys = jax.random.split(jax.random.fold_in(keys[6], part), 7)
    tokens = gaussian(own_keys[0], (TOKENS, D), 1.0, 6.0, ((0, 16),))
    route_keys = jax.random.split(jax.random.fold_in(own_keys[1], 1), TOKENS // TOK_DEV)
    route_turns = jax.random.permutation(jax.random.fold_in(own_keys[1], 3), TOKENS // TOK_DEV)
    route = jax.vmap(lambda own, number: routed_block(jax.random.fold_in(own_keys[1], 2), own, number, TOK_DEV, EXPERTS, TOPK, CAP, 2))(route_keys, route_turns).reshape((TOKENS, TOPK))
    gates = jnp.clip(0.2 + 1.3 * jax.random.uniform(own_keys[2], (TOKENS, TOPK), jnp.float32) ** shard_levels(own_keys[2], (TOKENS, TOPK), ((0, 16),), -0.2, 0.2), 0.2, 1.5)
    w_gate = gaussian(keys[3], (EXPERTS, D, FF), D ** -0.5, 0.0625, ((0, 4), (2, 4)))
    w_up = gaussian(keys[4], (EXPERTS, D, FF), D ** -0.5, 0.0625, ((0, 4), (2, 4)))
    w_down = gaussian(keys[5], (EXPERTS, FF, D), FF ** -0.5, 0.125, ((0, 4), (1, 4)))
    return {"tokens": tokens, "route": route, "gates": gates, "w_gate": w_gate, "w_up": w_up, "w_down": w_down}


def reference(tokens, route, gates, w_gate, w_up, w_down):
    flat_route = route.reshape(-1)
    flat_gates = gates.reshape(-1)
    bound = CAP * N_EX * N_EY
    slice_width = FF // N_EY

    def one_expert(mixed, expert):
        chosen = jnp.argsort((flat_route != expert).astype(jnp.int32), stable=True)[:bound].astype(jnp.int32)
        owners = (chosen // TOPK).astype(jnp.int32)
        picked = tokens[owners]
        pre_gate = jnp.dot(picked, w_gate[expert], preferred_element_type=jnp.float32)
        pre_up = jnp.dot(picked, w_up[expert], preferred_element_type=jnp.float32)
        hidden = (jax.nn.silu(pre_gate) * pre_up).astype(jnp.bfloat16)
        slice_terms = jnp.einsum("rsf,sfd->srd",
                                 hidden.reshape(bound, N_EY, slice_width).astype(jnp.float32),
                                 w_down[expert].reshape(N_EY, slice_width, D).astype(jnp.float32),
                                 precision=lax.Precision.HIGHEST)
        slice_terms = lax.optimization_barrier(slice_terms.astype(jnp.bfloat16)).astype(jnp.float32)
        expert_out = lax.optimization_barrier(jnp.sum(slice_terms, axis=0).astype(jnp.bfloat16)).astype(jnp.float32)
        share = jnp.where(flat_route[chosen] == expert, flat_gates[chosen], jnp.zeros_like(flat_gates[chosen]))
        mixed = mixed.at[owners].add(share[:, None] * expert_out)
        return mixed, None

    mixed, _ = lax.scan(one_expert, jnp.zeros((TOKENS, D), jnp.float32), jnp.arange(EXPERTS, dtype=jnp.int32))
    return mixed.astype(jnp.bfloat16)
```

```python
import functools

import jax
import jax.numpy as jnp
from jax import lax
from jax.experimental import pallas as pl
from jax.experimental.pallas import tpu as pltpu
from jax.sharding import PartitionSpec as P

F32 = jnp.float32
BF16 = jnp.bfloat16
ROWS = 16


def pick(shape, toks, inverse):
    n = shape[0]
    devs = n // ROWS
    q_of = ROWS // toks
    r = lax.broadcasted_iota(jnp.int32, shape, 1 if inverse else 0)
    k = lax.broadcasted_iota(jnp.int32, shape, 0 if inverse else 1)
    per_q = devs * toks
    q, rest = r // per_q, r % per_q
    want = (rest // toks) * (q_of * toks) + q * toks + rest % toks
    return jnp.where(want == k, 1.0, 0.0).astype(BF16)


def kernel(cfg, tok_ref, route_ref, gate_ref, wg_hbm, wu_hbm, wd_hbm, out_ref,
           wg, wu, wd, x, xa, acc_g, acc_u, y, r_sib, s1, r_x, s2, r_z,
           w_sem, ag_zs, ag_zr, ag_xs, ag_xr, ag_ss, ag_sr,
           rs_zs, rs_zr, rs_xs, rs_xr, rs_ss, rs_sr):
    nz, nx, chunks, w, toks, quarters = cfg
    ndev = 2 * nx * nz
    grp = min(ndev, 16)
    ngrp = ndev // grp
    quarter = chunks * w
    hid = wg.shape[2]
    z = lax.axis_index("ex")
    ey = lax.axis_index("ey")
    xi = ey // 2
    core = ey % 2

    def dev(zz, xx, cc):
        return {"ex": zz, "ey": xx * 2 + cc}

    def load_w(j):
        rows = pl.ds(j * w, w)
        return [pltpu.make_async_copy(wg_hbm.at[:, rows, :], wg.at[:, rows, :], w_sem.at[0, j]),
                pltpu.make_async_copy(wu_hbm.at[:, rows, :], wu.at[:, rows, :], w_sem.at[1, j])]

    def load_d(q):
        cols = pl.ds(q * quarter, quarter)
        return pltpu.make_async_copy(wd_hbm.at[:, cols], wd.at[:, cols], w_sem.at[2, q])

    for j in range(chunks):
        for c in load_w(j):
            c.start()
    for q in range(quarters):
        load_d(q).start()

    barrier = pltpu.get_barrier_semaphore()
    zs = [lax.rem(z + i, nz) for i in range(1, nz)]
    xs = [lax.rem(xi + i, nx) for i in range(1, nx)]
    for zz in zs:
        pl.semaphore_signal(barrier, inc=1, device_id=dev(zz, xi, core), device_id_type=pl.DeviceIdType.MESH)
    for xx in xs:
        pl.semaphore_signal(barrier, inc=1, device_id=dev(z, xx, core), device_id_type=pl.DeviceIdType.MESH)
    pl.semaphore_signal(barrier, inc=1, device_id=dev(z, xi, 1 - core), device_id_type=pl.DeviceIdType.MESH)

    t = tok_ref[...].astype(F32)
    for j in range(chunks):
        parts = [t[:, q * quarter + j * w:q * quarter + (j + 1) * w] for q in range(quarters)]
        x[j, core, xi, z] = jnp.concatenate(parts, axis=0).astype(BF16)
    rt = route_ref[...].astype(F32)
    gt = gate_ref[...]
    eye = lax.broadcasted_iota(jnp.int32, (toks, toks), 0) == lax.broadcasted_iota(jnp.int32, (toks, toks), 1)
    lane = lax.broadcasted_iota(jnp.int32, (toks, 128), 1).astype(F32)
    a = jnp.zeros((toks, 128), F32)
    for k in range(rt.shape[0]):
        rc = jnp.sum(jnp.where(eye, jnp.broadcast_to(rt[k:k + 1, :], (toks, toks)), 0.0), axis=1, keepdims=True)
        gc = jnp.sum(jnp.where(eye, jnp.broadcast_to(gt[k:k + 1, :], (toks, toks)), 0.0), axis=1, keepdims=True)
        a = a + jnp.where(lane == rc, gc, 0.0)
    hi = a.astype(BF16).astype(F32)
    mid = (a - hi).astype(BF16).astype(F32)
    low = a - hi - mid
    terms = [hi, mid, low] + [jnp.zeros_like(a)] * (quarters - 3)
    xa[core, xi, z] = jnp.concatenate(terms, axis=0).astype(BF16)

    pl.semaphore_wait(barrier, (nz - 1) + (nx - 1) + 1)

    def buf(j):
        return x.at[j] if j < chunks else xa

    def remote(src, dst, ss, rs, to):
        return pltpu.make_async_remote_copy(src_ref=src, dst_ref=dst, send_sem=ss, recv_sem=rs,
                                            device_id=to, device_id_type=pl.DeviceIdType.MESH)

    def ag_z(j, i, incoming=False):
        at = lax.rem(z + nz - i, nz) if incoming else z
        b = buf(j).at[core, xi, at]
        return remote(b, b, ag_zs.at[j, i], ag_zr.at[j, i], dev(lax.rem(z + i, nz), xi, core))

    def ag_x(j, i, incoming=False):
        at = lax.rem(xi + nx - i, nx) if incoming else xi
        b = buf(j).at[core, at]
        return remote(b, b, ag_xs.at[j, i], ag_xr.at[j, i], dev(z, lax.rem(xi + i, nx), core))

    def ag_s(j, incoming=False):
        b = buf(j).at[1 - core if incoming else core]
        return remote(b, b, ag_ss.at[j], ag_sr.at[j], dev(z, xi, 1 - core))

    order = list(range(chunks)) + [chunks]
    for j in order:
        for i in range(1, nz):
            ag_z(j, i).start()

    fwd = pick((grp * ROWS, grp * ROWS), toks, False)
    per_q = grp * toks

    def arrange(ref, width):
        whole = ref[...].reshape(ndev * ROWS, width)
        got = []
        for g in range(ngrp):
            got.append(jnp.dot(fwd, whole[g * grp * ROWS:(g + 1) * grp * ROWS], preferred_element_type=F32))
        return [jnp.concatenate([p[q * per_q:(q + 1) * per_q] for p in got], axis=0) for q in range(quarters)]

    def gate_up(j):
        for c in load_w(j):
            c.wait()
        rows = pl.ds(j * w, w)
        xc = jnp.concatenate([p.astype(BF16) for p in arrange(x.at[j], w)], axis=1)
        for acc, wt in ((acc_g, wg), (acc_u, wu)):
            d = jnp.dot(xc, wt[:, rows, :].reshape(quarters * w, hid), preferred_element_type=F32)
            acc[...] = d if j == 0 else acc[...] + d

    total = chunks + 1
    for i in range(total + 2):
        if i < total:
            for k in range(1, nz):
                ag_z(i, k, True).wait_recv()
            for k in range(1, nx):
                ag_x(i, k).start()
        if 0 <= i - 1 < total:
            for k in range(1, nx):
                ag_x(i - 1, k, True).wait_recv()
            ag_s(i - 1).start()
        if 0 <= i - 2 < total:
            ag_s(i - 2, True).wait_recv()
            if i - 2 < chunks:
                gate_up(i - 2)

    own = lax.broadcasted_iota(jnp.int32, (ndev * toks, 128), 1) == z
    aa = functools.reduce(lambda p, q: p + q, arrange(xa, 128)[:3])
    share = jnp.sum(jnp.where(own, aa, 0.0), axis=1, keepdims=True)
    g = acc_g[...]
    h = (g / (1.0 + jnp.exp(-g)) * acc_u[...]).astype(BF16)
    back = pick((grp * ROWS, grp * ROWS), toks, True)

    def rs_s(j):
        return remote(y.at[j, 1 - core], r_sib.at[j], rs_ss.at[j], rs_sr.at[j], dev(z, xi, 1 - core))

    def rs_x(j, i):
        return remote(s1.at[j, lax.rem(xi + i, nx)], r_x.at[j, i], rs_xs.at[j, i], rs_xr.at[j, i],
                      dev(z, lax.rem(xi + i, nx), core))

    def rs_z(j, i):
        return remote(s2.at[j, lax.rem(z + i, nz)], r_z.at[j, i], rs_zs.at[j, i], rs_zr.at[j, i],
                      dev(lax.rem(z + i, nz), xi, core))

    for q in range(quarters):
        load_d(q).wait()

    def down(j):
        terms = []
        for q in range(quarters):
            d = jnp.dot(h, wd[:, q * quarter + j * w:q * quarter + (j + 1) * w], preferred_element_type=F32)
            terms.append((d * share).astype(BF16))
        out = []
        for gi in range(ngrp):
            rows = jnp.concatenate([v[gi * per_q:(gi + 1) * per_q] for v in terms], axis=0)
            out.append(jnp.dot(back, rows, preferred_element_type=F32).astype(BF16))
        y[j] = jnp.concatenate(out, axis=0).reshape(2, nx, nz, ROWS, w)
        rs_s(j).start()

    def stage_x(j):
        rs_s(j).wait_recv()
        s1[j] = (y[j, core].astype(F32) + r_sib[j].astype(F32)).astype(BF16)
        for i in range(1, nx):
            rs_x(j, i).start()

    def stage_z(j):
        v = s1[j, xi].astype(F32)
        for i in range(1, nx):
            rs_x(j, i).wait_recv()
            v = v + r_x[j, i].astype(F32)
        s2[j] = v.astype(BF16)
        for i in range(1, nz):
            rs_z(j, i).start()

    def stage_out(j):
        v = s2[j, z].astype(F32)
        for i in range(1, nz):
            rs_z(j, i).wait_recv()
            v = v + r_z[j, i].astype(F32)
        for q in range(quarters):
            out_ref[:, q * quarter + j * w:q * quarter + (j + 1) * w] = v[q * toks:(q + 1) * toks].astype(BF16)

    stages = ((down, 0), (stage_x, 1), (stage_z, 2), (stage_out, 4))
    for i in range(chunks + 4):
        for fn, lag in stages:
            if 0 <= i - lag < chunks:
                fn(i - lag)

    for j in order:
        for i in range(1, nz):
            ag_z(j, i).wait_send()
        for i in range(1, nx):
            ag_x(j, i).wait_send()
        ag_s(j).wait_send()
    for j in range(chunks):
        for i in range(1, nz):
            rs_z(j, i).wait_send()
        for i in range(1, nx):
            rs_x(j, i).wait_send()
        rs_s(j).wait_send()


def chunk_count(quarter):
    lanes = quarter // 128
    return lanes // 2 if lanes % 2 == 0 else lanes


def on_device(tokens, route, gates, w_gate, w_up, w_down):
    nz = lax.axis_size("ex")
    nx = lax.axis_size("ey") // 2
    toks, width = tokens.shape
    quarters = ROWS // toks
    quarter = width // quarters
    hid = w_gate.shape[2]
    chunks = chunk_count(quarter)
    w = quarter // chunks
    ndev = 2 * nx * nz
    cfg = (nz, nx, chunks, w, toks, quarters)
    dma = pltpu.SemaphoreType.DMA
    vm = pl.BlockSpec(memory_space=pltpu.VMEM)
    hbm = pl.BlockSpec(memory_space=pl.ANY)
    return pl.pallas_call(
        functools.partial(kernel, cfg),
        out_shape=jax.ShapeDtypeStruct((toks, width), BF16),
        in_specs=[vm, vm, vm, hbm, hbm, hbm],
        out_specs=vm,
        scratch_shapes=[
            pltpu.VMEM((quarters, quarter, hid), BF16),
            pltpu.VMEM((quarters, quarter, hid), BF16),
            pltpu.VMEM((hid, width), BF16),
            pltpu.VMEM((chunks, 2, nx, nz, ROWS, w), BF16),
            pltpu.VMEM((2, nx, nz, ROWS, 128), BF16),
            pltpu.VMEM((ndev * toks, hid), F32),
            pltpu.VMEM((ndev * toks, hid), F32),
            pltpu.VMEM((chunks, 2, nx, nz, ROWS, w), BF16),
            pltpu.VMEM((chunks, nx, nz, ROWS, w), BF16),
            pltpu.VMEM((chunks, nx, nz, ROWS, w), BF16),
            pltpu.VMEM((chunks, nx, nz, ROWS, w), BF16),
            pltpu.VMEM((chunks, nz, ROWS, w), BF16),
            pltpu.VMEM((chunks, nz, ROWS, w), BF16),
            dma((3, max(chunks, quarters))),
            dma((chunks + 1, nz)), dma((chunks + 1, nz)),
            dma((chunks + 1, nx)), dma((chunks + 1, nx)),
            dma((chunks + 1,)), dma((chunks + 1,)),
            dma((chunks, nz)), dma((chunks, nz)),
            dma((chunks, nx)), dma((chunks, nx)),
            dma((chunks,)), dma((chunks,)),
        ],
        compiler_params=pltpu.CompilerParams(
            collective_id=0, has_side_effects=True, vmem_limit_bytes=56 * 1024 * 1024
        ),
    )(tokens, route.T, gates.T, w_gate.reshape(quarters, quarter, hid),
      w_up.reshape(quarters, quarter, hid), w_down[0])


def solution(mesh):
    placed = (
        P(("groups", "ex", "ey"), None),
        P(("groups", "ex", "ey"), None),
        P(("groups", "ex", "ey"), None),
        P("ex", None, "ey"),
        P("ex", None, "ey"),
        P("ex", "ey", None),
    )
    return jax.shard_map(
        on_device,
        mesh=mesh,
        in_specs=placed,
        out_specs=P(("groups", "ex", "ey"), None),
        check_vma=False,
    )
```

```python
import functools

import jax
import jax.numpy as jnp
from jax import lax
from jax.experimental import pallas as pl
from jax.experimental.pallas import tpu as pltpu
from jax.sharding import PartitionSpec as P

F32 = jnp.float32
BF16 = jnp.bfloat16
ROWS = 16


def pick(shape, toks, inverse):
    n = shape[0]
    devs = n // ROWS
    q_of = ROWS // toks
    r = lax.broadcasted_iota(jnp.int32, shape, 1 if inverse else 0)
    k = lax.broadcasted_iota(jnp.int32, shape, 0 if inverse else 1)
    per_q = devs * toks
    q, rest = r // per_q, r % per_q
    want = (rest // toks) * (q_of * toks) + q * toks + rest % toks
    return jnp.where(want == k, 1.0, 0.0).astype(BF16)


def kernel(cfg, tok_ref, route_ref, gate_ref, wg_hbm, wu_hbm, wd_hbm, out_ref,
           wg, wu, wd, x, xa, acc_g, acc_u, y, r_sib, s1, r_x, s2, r_z,
           w_sem, ag_zs, ag_zr, ag_xs, ag_xr, ag_ss, ag_sr,
           rs_zs, rs_zr, rs_xs, rs_xr, rs_ss, rs_sr):
    nz, nx, widths, toks, quarters = cfg
    ndev = 2 * nx * nz
    grp = min(ndev, 16)
    ngrp = ndev // grp
    chunks = len(widths)
    quarter = sum(widths)
    starts = [sum(widths[:j]) for j in range(chunks)]
    hid = wg.shape[2]
    z = lax.axis_index("ex")
    ey = lax.axis_index("ey")
    xi = ey // 2
    core = ey % 2

    def lanes(q, j):
        return slice(q * quarter + starts[j], q * quarter + starts[j] + widths[j])

    def dev(zz, xx, cc):
        return {"ex": zz, "ey": xx * 2 + cc}

    def load_w(j):
        rows = pl.ds(starts[j], widths[j])
        return [pltpu.make_async_copy(wg_hbm.at[:, rows, :], wg.at[:, rows, :], w_sem.at[0, j]),
                pltpu.make_async_copy(wu_hbm.at[:, rows, :], wu.at[:, rows, :], w_sem.at[1, j])]

    def load_d(q):
        cols = pl.ds(q * quarter, quarter)
        return pltpu.make_async_copy(wd_hbm.at[:, cols], wd.at[:, cols], w_sem.at[2, q])

    for j in range(chunks):
        for c in load_w(j):
            c.start()
    for q in range(quarters):
        load_d(q).start()

    barrier = pltpu.get_barrier_semaphore()
    zs = [lax.rem(z + i, nz) for i in range(1, nz)]
    xs = [lax.rem(xi + i, nx) for i in range(1, nx)]
    for zz in zs:
        pl.semaphore_signal(barrier, inc=1, device_id=dev(zz, xi, core), device_id_type=pl.DeviceIdType.MESH)
    for xx in xs:
        pl.semaphore_signal(barrier, inc=1, device_id=dev(z, xx, core), device_id_type=pl.DeviceIdType.MESH)
    pl.semaphore_signal(barrier, inc=1, device_id=dev(z, xi, 1 - core), device_id_type=pl.DeviceIdType.MESH)

    t = tok_ref[...].astype(F32)
    for j in range(chunks):
        parts = [t[:, lanes(q, j)] for q in range(quarters)]
        x[j][core, xi, z] = jnp.concatenate(parts, axis=0).astype(BF16)
    rt = route_ref[...].astype(F32)
    gt = gate_ref[...]
    eye = lax.broadcasted_iota(jnp.int32, (toks, toks), 0) == lax.broadcasted_iota(jnp.int32, (toks, toks), 1)
    lane = lax.broadcasted_iota(jnp.int32, (toks, 128), 1).astype(F32)
    a = jnp.zeros((toks, 128), F32)
    for k in range(rt.shape[0]):
        rc = jnp.sum(jnp.where(eye, jnp.broadcast_to(rt[k:k + 1, :], (toks, toks)), 0.0), axis=1, keepdims=True)
        gc = jnp.sum(jnp.where(eye, jnp.broadcast_to(gt[k:k + 1, :], (toks, toks)), 0.0), axis=1, keepdims=True)
        a = a + jnp.where(lane == rc, gc, 0.0)
    hi = a.astype(BF16).astype(F32)
    mid = (a - hi).astype(BF16).astype(F32)
    low = a - hi - mid
    terms = [hi, mid, low] + [jnp.zeros_like(a)] * (quarters - 3)
    xa[core, xi, z] = jnp.concatenate(terms, axis=0).astype(BF16)

    pl.semaphore_wait(barrier, (nz - 1) + (nx - 1) + 1)

    def buf(j):
        return x[j] if j < chunks else xa

    def remote(src, dst, ss, rs, to):
        return pltpu.make_async_remote_copy(src_ref=src, dst_ref=dst, send_sem=ss, recv_sem=rs,
                                            device_id=to, device_id_type=pl.DeviceIdType.MESH)

    last = chunks - 1

    def ag_z(j, i, incoming=False):
        at = lax.rem(z + nz - i, nz) if incoming else z
        b = buf(j).at[core, :, at] if j == last else buf(j).at[core, xi, at]
        return remote(b, b, ag_zs.at[j, i], ag_zr.at[j, i], dev(lax.rem(z + i, nz), xi, core))

    def ag_x(j, i, incoming=False):
        at = lax.rem(xi + nx - i, nx) if incoming else xi
        b = buf(j).at[core, at, z] if j == last else buf(j).at[core, at]
        return remote(b, b, ag_xs.at[j, i], ag_xr.at[j, i], dev(z, lax.rem(xi + i, nx), core))

    def ag_s(j, incoming=False):
        b = buf(j).at[1 - core if incoming else core]
        return remote(b, b, ag_ss.at[j], ag_sr.at[j], dev(z, xi, 1 - core))

    def hops(first, j):
        along_z = first != (j == last)
        return (ag_z, nz) if along_z else (ag_x, nx)

    order = list(range(chunks)) + [chunks]
    for j in order:
        fn, n = hops(True, j)
        for i in range(1, n):
            fn(j, i).start()

    fwd = pick((grp * ROWS, grp * ROWS), toks, False)
    per_q = grp * toks

    def arrange(ref, width):
        whole = ref[...].reshape(ndev * ROWS, width)
        got = []
        for g in range(ngrp):
            got.append(jnp.dot(fwd, whole[g * grp * ROWS:(g + 1) * grp * ROWS], preferred_element_type=F32))
        return [jnp.concatenate([p[q * per_q:(q + 1) * per_q] for p in got], axis=0) for q in range(quarters)]

    def gate_up(j):
        for c in load_w(j):
            c.wait()
        rows = pl.ds(starts[j], widths[j])
        xc = jnp.concatenate([p.astype(BF16) for p in arrange(x[j], widths[j])], axis=1)
        for acc, wt in ((acc_g, wg), (acc_u, wu)):
            d = jnp.dot(xc, wt[:, rows, :].reshape(quarters * widths[j], hid), preferred_element_type=F32)
            acc[...] = d if j == 0 else acc[...] + d

    for j in [last] + [j for j in order if j != last]:
        fn, n = hops(True, j)
        for i in range(1, n):
            fn(j, i, True).wait_recv()
        fn, n = hops(False, j)
        for i in range(1, n):
            fn(j, i).start()
    for j in order:
        fn, n = hops(False, j)
        for i in range(1, n):
            fn(j, i, True).wait_recv()
        ag_s(j).start()
    for j in order:
        ag_s(j, True).wait_recv()
        if j < chunks:
            gate_up(j)

    own = lax.broadcasted_iota(jnp.int32, (ndev * toks, 128), 1) == z
    aa = functools.reduce(lambda p, q: p + q, arrange(xa, 128)[:3])
    share = jnp.sum(jnp.where(own, aa, 0.0), axis=1, keepdims=True)
    g = acc_g[...]
    h = (g / (1.0 + jnp.exp(-g)) * acc_u[...]).astype(BF16)
    back = pick((grp * ROWS, grp * ROWS), toks, True)

    def rs_s(j):
        return remote(y[j].at[1 - core], r_sib[j], rs_ss.at[j], rs_sr.at[j], dev(z, xi, 1 - core))

    def rs_x(j, i):
        to = lax.rem(xi + i, nx)
        src = s2[j].at[to] if j == last else s1[j].at[to]
        return remote(src, r_x[j].at[i], rs_xs.at[j, i], rs_xr.at[j, i], dev(z, to, core))

    def rs_z(j, i):
        to = lax.rem(z + i, nz)
        src = s1[j].at[:, to] if j == last else s2[j].at[to]
        return remote(src, r_z[j].at[i], rs_zs.at[j, i], rs_zr.at[j, i], dev(to, xi, core))

    for q in range(quarters):
        load_d(q).wait()

    def down(j):
        terms = []
        for q in range(quarters):
            d = jnp.dot(h, wd[:, lanes(q, j)], preferred_element_type=F32)
            terms.append((d * share).astype(BF16))
        out = []
        for gi in range(ngrp):
            rows = jnp.concatenate([v[gi * per_q:(gi + 1) * per_q] for v in terms], axis=0)
            out.append(jnp.dot(back, rows, preferred_element_type=F32).astype(BF16))
        y[j][...] = jnp.concatenate(out, axis=0).reshape(2, nx, nz, ROWS, widths[j])
        rs_s(j).start()

    def first_hop(j):
        rs_s(j).wait_recv()
        s1[j][...] = (y[j][core].astype(F32) + r_sib[j][...].astype(F32)).astype(BF16)
        fn, n = (rs_z, nz) if j == last else (rs_x, nx)
        for i in range(1, n):
            fn(j, i).start()

    def second_hop(j):
        if j == last:
            v = s1[j][:, z].astype(F32)
            for i in range(1, nz):
                rs_z(j, i).wait_recv()
                v = v + r_z[j][i].astype(F32)
        else:
            v = s1[j][xi].astype(F32)
            for i in range(1, nx):
                rs_x(j, i).wait_recv()
                v = v + r_x[j][i].astype(F32)
        s2[j][...] = v.astype(BF16)
        fn, n = (rs_x, nx) if j == last else (rs_z, nz)
        for i in range(1, n):
            fn(j, i).start()

    def stage_out(j):
        if j == last:
            v = s2[j][xi].astype(F32)
            for i in range(1, nx):
                rs_x(j, i).wait_recv()
                v = v + r_x[j][i].astype(F32)
        else:
            v = s2[j][z].astype(F32)
            for i in range(1, nz):
                rs_z(j, i).wait_recv()
                v = v + r_z[j][i].astype(F32)
        for q in range(quarters):
            out_ref[:, lanes(q, j)] = v[q * toks:(q + 1) * toks].astype(BF16)

    turns = [last] + list(range(last))
    for fn in (down, first_hop):
        for j in turns:
            fn(j)
    for fn in (second_hop, stage_out):
        for j in turns[::-1] if fn is second_hop else turns:
            fn(j)

    for j in order:
        for i in range(1, nz):
            ag_z(j, i).wait_send()
        for i in range(1, nx):
            ag_x(j, i).wait_send()
        ag_s(j).wait_send()
    for j in range(chunks):
        for i in range(1, nz):
            rs_z(j, i).wait_send()
        for i in range(1, nx):
            rs_x(j, i).wait_send()
        rs_s(j).wait_send()


def chunk_widths(quarter):
    n = quarter // 128
    small = max(1, (n * 6) // 14)
    return ((n - small) * 128, small * 128)


def on_device(tokens, route, gates, w_gate, w_up, w_down):
    nz = lax.axis_size("ex")
    nx = lax.axis_size("ey") // 2
    toks, width = tokens.shape
    quarters = ROWS // toks
    quarter = width // quarters
    hid = w_gate.shape[2]
    widths = chunk_widths(quarter)
    chunks = len(widths)
    last = chunks - 1
    ndev = 2 * nx * nz
    cfg = (nz, nx, widths, toks, quarters)
    dma = pltpu.SemaphoreType.DMA

    def per_chunk(lead):
        return [pltpu.VMEM(lead(j) + (ROWS, widths[j]), BF16) for j in range(chunks)]

    vm = pl.BlockSpec(memory_space=pltpu.VMEM)
    hbm = pl.BlockSpec(memory_space=pl.ANY)
    return pl.pallas_call(
        functools.partial(kernel, cfg),
        out_shape=jax.ShapeDtypeStruct((toks, width), BF16),
        in_specs=[vm, vm, vm, hbm, hbm, hbm],
        out_specs=vm,
        scratch_shapes=[
            pltpu.VMEM((quarters, quarter, hid), BF16),
            pltpu.VMEM((quarters, quarter, hid), BF16),
            pltpu.VMEM((hid, width), BF16),
            per_chunk(lambda j: (2, nx, nz)),
            pltpu.VMEM((2, nx, nz, ROWS, 128), BF16),
            pltpu.VMEM((ndev * toks, hid), F32),
            pltpu.VMEM((ndev * toks, hid), F32),
            per_chunk(lambda j: (2, nx, nz)),
            per_chunk(lambda j: (nx, nz)),
            per_chunk(lambda j: (nx, nz)),
            per_chunk(lambda j: (nx,) if j == last else (nx, nz)),
            per_chunk(lambda j: (nx,) if j == last else (nz,)),
            per_chunk(lambda j: (nz, nx) if j == last else (nz,)),
            dma((3, max(chunks, quarters))),
            dma((chunks + 1, nz)), dma((chunks + 1, nz)),
            dma((chunks + 1, nx)), dma((chunks + 1, nx)),
            dma((chunks + 1,)), dma((chunks + 1,)),
            dma((chunks, nz)), dma((chunks, nz)),
            dma((chunks, nx)), dma((chunks, nx)),
            dma((chunks,)), dma((chunks,)),
        ],
        compiler_params=pltpu.CompilerParams(
            collective_id=0, has_side_effects=True, vmem_limit_bytes=56 * 1024 * 1024
        ),
    )(tokens, route.T, gates.T, w_gate.reshape(quarters, quarter, hid),
      w_up.reshape(quarters, quarter, hid), w_down[0])


def solution(mesh):
    placed = (
        P(("groups", "ex", "ey"), None),
        P(("groups", "ex", "ey"), None),
        P(("groups", "ex", "ey"), None),
        P("ex", None, "ey"),
        P("ex", None, "ey"),
        P("ex", "ey", None),
    )
    return jax.shard_map(
        on_device,
        mesh=mesh,
        in_specs=placed,
        out_specs=P(("groups", "ex", "ey"), None),
        check_vma=False,
    )
```

```python
import functools

import jax
import jax.numpy as jnp
from jax import lax
from jax.experimental import pallas as pl
from jax.experimental.pallas import tpu as pltpu
from jax.sharding import PartitionSpec as P

F32 = jnp.float32
BF16 = jnp.bfloat16
ROWS = 16


def pick(shape, toks, inverse):
    n = shape[0]
    devs = n // ROWS
    q_of = ROWS // toks
    r = lax.broadcasted_iota(jnp.int32, shape, 1 if inverse else 0)
    k = lax.broadcasted_iota(jnp.int32, shape, 0 if inverse else 1)
    per_q = devs * toks
    q, rest = r // per_q, r % per_q
    want = (rest // toks) * (q_of * toks) + q * toks + rest % toks
    return jnp.where(want == k, 1.0, 0.0).astype(BF16)


def kernel(cfg, tok_ref, route_ref, gate_ref, wg_hbm, wu_hbm, wd_hbm, out_ref,
           wg, wu, wd, x, acc_g, acc_u, y, r_sib, s1, r_x, s2, r_z,
           w_sem, ag_zs, ag_zr, ag_xs, ag_xr, ag_ss, ag_sr,
           rs_zs, rs_zr, rs_xs, rs_xr, rs_ss, rs_sr):
    nz, nx, widths, toks, quarters = cfg
    ndev = 2 * nx * nz
    grp = min(ndev, 16)
    ngrp = ndev // grp
    chunks = len(widths)
    quarter = sum(widths)
    starts = [sum(widths[:j]) for j in range(chunks)]
    hid = wg.shape[2]
    z = lax.axis_index("ex")
    ey = lax.axis_index("ey")
    xi = ey // 2
    core = ey % 2

    def lanes(q, j):
        return slice(q * quarter + starts[j], q * quarter + starts[j] + widths[j])

    def dev(zz, xx, cc):
        return {"ex": zz, "ey": xx * 2 + cc}

    def load_w(j):
        rows = pl.ds(starts[j], widths[j])
        return [pltpu.make_async_copy(wg_hbm.at[:, rows, :], wg.at[:, rows, :], w_sem.at[0, j]),
                pltpu.make_async_copy(wu_hbm.at[:, rows, :], wu.at[:, rows, :], w_sem.at[1, j])]

    def load_d(q):
        cols = pl.ds(q * quarter, quarter)
        return pltpu.make_async_copy(wd_hbm.at[:, cols], wd.at[:, cols], w_sem.at[2, q])

    for j in range(chunks):
        for c in load_w(j):
            c.start()
    for q in range(quarters):
        load_d(q).start()

    barrier = pltpu.get_barrier_semaphore()
    zs = [lax.rem(z + i, nz) for i in range(1, nz)]
    xs = [lax.rem(xi + i, nx) for i in range(1, nx)]
    for zz in zs:
        pl.semaphore_signal(barrier, inc=1, device_id=dev(zz, xi, core), device_id_type=pl.DeviceIdType.MESH)
    for xx in xs:
        pl.semaphore_signal(barrier, inc=1, device_id=dev(z, xx, core), device_id_type=pl.DeviceIdType.MESH)
    pl.semaphore_signal(barrier, inc=1, device_id=dev(z, xi, 1 - core), device_id_type=pl.DeviceIdType.MESH)

    t = tok_ref[...].astype(F32)
    for j in range(chunks):
        parts = [t[:, lanes(q, j)] for q in range(quarters)]
        x[j][core, xi, z, :, :widths[j]] = jnp.concatenate(parts, axis=0).astype(BF16)
    rt = route_ref[...].astype(F32)
    gt = gate_ref[...]
    eye = lax.broadcasted_iota(jnp.int32, (toks, toks), 0) == lax.broadcasted_iota(jnp.int32, (toks, toks), 1)
    lane = lax.broadcasted_iota(jnp.int32, (toks, 128), 1).astype(F32)
    a = jnp.zeros((toks, 128), F32)
    for k in range(rt.shape[0]):
        rc = jnp.sum(jnp.where(eye, jnp.broadcast_to(rt[k:k + 1, :], (toks, toks)), 0.0), axis=1, keepdims=True)
        gc = jnp.sum(jnp.where(eye, jnp.broadcast_to(gt[k:k + 1, :], (toks, toks)), 0.0), axis=1, keepdims=True)
        a = a + jnp.where(lane == rc, gc, 0.0)
    hi = a.astype(BF16).astype(F32)
    mid = (a - hi).astype(BF16).astype(F32)
    low = a - hi - mid
    terms = [hi, mid, low] + [jnp.zeros_like(a)] * (quarters - 3)
    x[-1][core, xi, z, :, widths[-1]:] = jnp.concatenate(terms, axis=0).astype(BF16)

    pl.semaphore_wait(barrier, (nz - 1) + (nx - 1) + 1)

    def remote(src, dst, ss, rs, to):
        return pltpu.make_async_remote_copy(src_ref=src, dst_ref=dst, send_sem=ss, recv_sem=rs,
                                            device_id=to, device_id_type=pl.DeviceIdType.MESH)

    last = chunks - 1

    def ag_z(j, i, incoming=False):
        at = lax.rem(z + nz - i, nz) if incoming else z
        b = x[j].at[core, :, at] if j == last else x[j].at[core, xi, at]
        return remote(b, b, ag_zs.at[j, i], ag_zr.at[j, i], dev(lax.rem(z + i, nz), xi, core))

    def ag_x(j, i, incoming=False):
        at = lax.rem(xi + nx - i, nx) if incoming else xi
        b = x[j].at[core, at, z] if j == last else x[j].at[core, at]
        return remote(b, b, ag_xs.at[j, i], ag_xr.at[j, i], dev(z, lax.rem(xi + i, nx), core))

    def ag_s(j, incoming=False):
        b = x[j].at[1 - core if incoming else core]
        return remote(b, b, ag_ss.at[j], ag_sr.at[j], dev(z, xi, 1 - core))

    def hops(first, j):
        along_z = first != (j == last)
        return (ag_z, nz) if along_z else (ag_x, nx)

    order = list(range(chunks))
    for j in order:
        fn, n = hops(True, j)
        for i in range(1, n):
            fn(j, i).start()

    fwd = pick((grp * ROWS, grp * ROWS), toks, False)
    per_q = grp * toks

    def arrange(ref, width):
        whole = ref[...].reshape(ndev * ROWS, width)
        got = []
        for g in range(ngrp):
            got.append(jnp.dot(fwd, whole[g * grp * ROWS:(g + 1) * grp * ROWS], preferred_element_type=F32))
        return [jnp.concatenate([p[q * per_q:(q + 1) * per_q] for p in got], axis=0) for q in range(quarters)]

    def gate_up(j):
        for c in load_w(j):
            c.wait()
        rows = pl.ds(starts[j], widths[j])
        parts = arrange(x[j], x[j].shape[-1])
        xc = jnp.concatenate([p[:, :widths[j]].astype(BF16) for p in parts], axis=1)
        for acc, wt in ((acc_g, wg), (acc_u, wu)):
            d = jnp.dot(xc, wt[:, rows, :].reshape(quarters * widths[j], hid), preferred_element_type=F32)
            acc[...] = d if j == 0 else acc[...] + d
        return parts

    for j in [last] + [j for j in order if j != last]:
        fn, n = hops(True, j)
        for i in range(1, n):
            fn(j, i, True).wait_recv()
        fn, n = hops(False, j)
        for i in range(1, n):
            fn(j, i).start()
    for j in order:
        fn, n = hops(False, j)
        for i in range(1, n):
            fn(j, i, True).wait_recv()
        ag_s(j).start()
    for j in order:
        ag_s(j, True).wait_recv()
        parts = gate_up(j)

    own = lax.broadcasted_iota(jnp.int32, (ndev * toks, 128), 1) == z
    aa = functools.reduce(lambda p, q: p + q, [p[:, widths[last]:] for p in parts[:3]])
    share = jnp.sum(jnp.where(own, aa, 0.0), axis=1, keepdims=True)
    g = acc_g[...]
    h = (g / (1.0 + jnp.exp(-g)) * acc_u[...]).astype(BF16)
    back = pick((grp * ROWS, grp * ROWS), toks, True)

    def rs_s(j):
        return remote(y[j].at[1 - core], r_sib[j], rs_ss.at[j], rs_sr.at[j], dev(z, xi, 1 - core))

    def rs_x(j, i):
        to = lax.rem(xi + i, nx)
        src = s2[j].at[to] if j == last else s1[j].at[to]
        return remote(src, r_x[j].at[i], rs_xs.at[j, i], rs_xr.at[j, i], dev(z, to, core))

    def rs_z(j, i):
        to = lax.rem(z + i, nz)
        src = s1[j].at[:, to] if j == last else s2[j].at[to]
        return remote(src, r_z[j].at[i], rs_zs.at[j, i], rs_zr.at[j, i], dev(to, xi, core))

    for q in range(quarters):
        load_d(q).wait()

    def down(j):
        terms = []
        for q in range(quarters):
            d = jnp.dot(h, wd[:, lanes(q, j)], preferred_element_type=F32)
            terms.append((d * share).astype(BF16))
        out = []
        for gi in range(ngrp):
            rows = jnp.concatenate([v[gi * per_q:(gi + 1) * per_q] for v in terms], axis=0)
            out.append(jnp.dot(back, rows, preferred_element_type=F32).astype(BF16))
        y[j][...] = jnp.concatenate(out, axis=0).reshape(2, nx, nz, ROWS, widths[j])
        rs_s(j).start()

    def first_hop(j):
        rs_s(j).wait_recv()
        s1[j][...] = (y[j][core].astype(F32) + r_sib[j][...].astype(F32)).astype(BF16)
        fn, n = (rs_z, nz) if j == last else (rs_x, nx)
        for i in range(1, n):
            fn(j, i).start()

    def second_hop(j):
        if j == last:
            v = s1[j][:, z].astype(F32)
            for i in range(1, nz):
                rs_z(j, i).wait_recv()
                v = v + r_z[j][i].astype(F32)
        else:
            v = s1[j][xi].astype(F32)
            for i in range(1, nx):
                rs_x(j, i).wait_recv()
                v = v + r_x[j][i].astype(F32)
        s2[j][...] = v.astype(BF16)
        fn, n = (rs_x, nx) if j == last else (rs_z, nz)
        for i in range(1, n):
            fn(j, i).start()

    def stage_out(j):
        if j == last:
            v = s2[j][xi].astype(F32)
            for i in range(1, nx):
                rs_x(j, i).wait_recv()
                v = v + r_x[j][i].astype(F32)
        else:
            v = s2[j][z].astype(F32)
            for i in range(1, nz):
                rs_z(j, i).wait_recv()
                v = v + r_z[j][i].astype(F32)
        for q in range(quarters):
            out_ref[:, lanes(q, j)] = v[q * toks:(q + 1) * toks].astype(BF16)

    turns = [last] + list(range(last))
    for fn in (down, first_hop):
        for j in turns:
            fn(j)
    for fn in (second_hop, stage_out):
        for j in turns[::-1] if fn is second_hop else turns:
            fn(j)

    for j in order:
        for i in range(1, nz):
            ag_z(j, i).wait_send()
        for i in range(1, nx):
            ag_x(j, i).wait_send()
        ag_s(j).wait_send()
    for j in range(chunks):
        for i in range(1, nz):
            rs_z(j, i).wait_send()
        for i in range(1, nx):
            rs_x(j, i).wait_send()
        rs_s(j).wait_send()


def chunk_widths(quarter):
    n = quarter // 128
    small = max(1, (n * 6) // 14)
    return ((n - small) * 128, small * 128)


def on_device(tokens, route, gates, w_gate, w_up, w_down):
    nz = lax.axis_size("ex")
    nx = lax.axis_size("ey") // 2
    toks, width = tokens.shape
    quarters = ROWS // toks
    quarter = width // quarters
    hid = w_gate.shape[2]
    widths = chunk_widths(quarter)
    chunks = len(widths)
    last = chunks - 1
    ndev = 2 * nx * nz
    cfg = (nz, nx, widths, toks, quarters)
    dma = pltpu.SemaphoreType.DMA

    def per_chunk(lead, extra=0):
        return [pltpu.VMEM(lead(j) + (ROWS, widths[j] + (extra if j == last else 0)), BF16) for j in range(chunks)]

    vm = pl.BlockSpec(memory_space=pltpu.VMEM)
    hbm = pl.BlockSpec(memory_space=pl.ANY)
    return pl.pallas_call(
        functools.partial(kernel, cfg),
        out_shape=jax.ShapeDtypeStruct((toks, width), BF16),
        in_specs=[vm, vm, vm, hbm, hbm, hbm],
        out_specs=vm,
        scratch_shapes=[
            pltpu.VMEM((quarters, quarter, hid), BF16),
            pltpu.VMEM((quarters, quarter, hid), BF16),
            pltpu.VMEM((hid, width), BF16),
            per_chunk(lambda j: (2, nx, nz), 128),
            pltpu.VMEM((ndev * toks, hid), F32),
            pltpu.VMEM((ndev * toks, hid), F32),
            per_chunk(lambda j: (2, nx, nz)),
            per_chunk(lambda j: (nx, nz)),
            per_chunk(lambda j: (nx, nz)),
            per_chunk(lambda j: (nx,) if j == last else (nx, nz)),
            per_chunk(lambda j: (nx,) if j == last else (nz,)),
            per_chunk(lambda j: (nz, nx) if j == last else (nz,)),
            dma((3, max(chunks, quarters))),
            dma((chunks, nz)), dma((chunks, nz)),
            dma((chunks, nx)), dma((chunks, nx)),
            dma((chunks,)), dma((chunks,)),
            dma((chunks, nz)), dma((chunks, nz)),
            dma((chunks, nx)), dma((chunks, nx)),
            dma((chunks,)), dma((chunks,)),
        ],
        compiler_params=pltpu.CompilerParams(
            collective_id=0, has_side_effects=True, vmem_limit_bytes=56 * 1024 * 1024
        ),
    )(tokens, route.T, gates.T, w_gate.reshape(quarters, quarter, hid),
      w_up.reshape(quarters, quarter, hid), w_down[0])


def solution(mesh):
    placed = (
        P(("groups", "ex", "ey"), None),
        P(("groups", "ex", "ey"), None),
        P(("groups", "ex", "ey"), None),
        P("ex", None, "ey"),
        P("ex", None, "ey"),
        P("ex", "ey", None),
    )
    return jax.shard_map(
        on_device,
        mesh=mesh,
        in_specs=placed,
        out_specs=P(("groups", "ex", "ey"), None),
        check_vma=False,
    )
```

```python
import functools

import jax
import jax.numpy as jnp
from jax import lax
from jax.experimental import pallas as pl
from jax.experimental.pallas import tpu as pltpu
from jax.sharding import PartitionSpec as P

F32 = jnp.float32
BF16 = jnp.bfloat16
ROWS = 16


def pick(shape, toks, inverse):
    n = shape[0]
    devs = n // ROWS
    q_of = ROWS // toks
    r = lax.broadcasted_iota(jnp.int32, shape, 1 if inverse else 0)
    k = lax.broadcasted_iota(jnp.int32, shape, 0 if inverse else 1)
    per_q = devs * toks
    q, rest = r // per_q, r % per_q
    want = (rest // toks) * (q_of * toks) + q * toks + rest % toks
    return jnp.where(want == k, 1.0, 0.0).astype(BF16)


def kernel(cfg, tok_ref, route_ref, gate_ref, wg_hbm, wu_hbm, wd_hbm, out_ref,
           wg, wu, wd, x, xa, acc_g, acc_u, y, r_sib, s1, r_x, s2, r_z,
           w_sem, ag_zs, ag_zr, ag_xs, ag_xr, ag_ss, ag_sr,
           rs_zs, rs_zr, rs_xs, rs_xr, rs_ss, rs_sr):
    nz, nx, widths, toks, quarters = cfg
    ndev = 2 * nx * nz
    grp = min(ndev, 16)
    ngrp = ndev // grp
    chunks = len(widths)
    quarter = sum(widths)
    starts = [sum(widths[:j]) for j in range(chunks)]
    hid = wg.shape[2]
    z = lax.axis_index("ex")
    ey = lax.axis_index("ey")
    xi = ey // 2
    core = ey % 2

    def lanes(q, j):
        return slice(q * quarter + starts[j], q * quarter + starts[j] + widths[j])

    def dev(zz, xx, cc):
        return {"ex": zz, "ey": xx * 2 + cc}

    def load_w(j):
        rows = pl.ds(starts[j], widths[j])
        return [pltpu.make_async_copy(wg_hbm.at[:, rows, :], wg.at[:, rows, :], w_sem.at[0, j]),
                pltpu.make_async_copy(wu_hbm.at[:, rows, :], wu.at[:, rows, :], w_sem.at[1, j])]

    def load_d(q):
        cols = pl.ds(q * quarter, quarter)
        return pltpu.make_async_copy(wd_hbm.at[:, cols], wd.at[:, cols], w_sem.at[2, q])

    barrier = pltpu.get_barrier_semaphore()
    zs = [lax.rem(z + i, nz) for i in range(1, nz)]
    xs = [lax.rem(xi + i, nx) for i in range(1, nx)]
    for zz in zs:
        pl.semaphore_signal(barrier, inc=1, device_id=dev(zz, xi, core), device_id_type=pl.DeviceIdType.MESH)
    for xx in xs:
        pl.semaphore_signal(barrier, inc=1, device_id=dev(z, xx, core), device_id_type=pl.DeviceIdType.MESH)
    pl.semaphore_signal(barrier, inc=1, device_id=dev(z, xi, 1 - core), device_id_type=pl.DeviceIdType.MESH)

    for j in range(chunks):
        for c in load_w(j):
            c.start()
    for q in range(quarters):
        load_d(q).start()

    t = tok_ref[...].astype(F32)
    for j in range(chunks):
        parts = [t[:, lanes(q, j)] for q in range(quarters)]
        x[j][core, xi, z] = jnp.concatenate(parts, axis=0).astype(BF16)
    rt = route_ref[...].astype(F32)
    gt = gate_ref[...]
    eye = lax.broadcasted_iota(jnp.int32, (toks, toks), 0) == lax.broadcasted_iota(jnp.int32, (toks, toks), 1)
    lane = lax.broadcasted_iota(jnp.int32, (toks, 128), 1).astype(F32)
    a = jnp.zeros((toks, 128), F32)
    for k in range(rt.shape[0]):
        rc = jnp.sum(jnp.where(eye, jnp.broadcast_to(rt[k:k + 1, :], (toks, toks)), 0.0), axis=1, keepdims=True)
        gc = jnp.sum(jnp.where(eye, jnp.broadcast_to(gt[k:k + 1, :], (toks, toks)), 0.0), axis=1, keepdims=True)
        a = a + jnp.where(lane == rc, gc, 0.0)
    hi = a.astype(BF16).astype(F32)
    mid = (a - hi).astype(BF16).astype(F32)
    low = a - hi - mid
    terms = [hi, mid, low] + [jnp.zeros_like(a)] * (quarters - 3)
    xa[core, xi, z] = jnp.concatenate(terms, axis=0).astype(BF16)

    pl.semaphore_wait(barrier, (nz - 1) + (nx - 1) + 1)

    def buf(j):
        return x[j] if j < chunks else xa

    def remote(src, dst, ss, rs, to):
        return pltpu.make_async_remote_copy(src_ref=src, dst_ref=dst, send_sem=ss, recv_sem=rs,
                                            device_id=to, device_id_type=pl.DeviceIdType.MESH)

    last = chunks - 1

    def ag_z(j, i, incoming=False):
        at = lax.rem(z + nz - i, nz) if incoming else z
        b = buf(j).at[core, :, at] if j == last else buf(j).at[core, xi, at]
        return remote(b, b, ag_zs.at[j, i], ag_zr.at[j, i], dev(lax.rem(z + i, nz), xi, core))

    def ag_x(j, i, incoming=False):
        at = lax.rem(xi + nx - i, nx) if incoming else xi
        b = buf(j).at[core, at, z] if j == last else buf(j).at[core, at]
        return remote(b, b, ag_xs.at[j, i], ag_xr.at[j, i], dev(z, lax.rem(xi + i, nx), core))

    def ag_s(j, incoming=False):
        b = buf(j).at[1 - core if incoming else core]
        return remote(b, b, ag_ss.at[j], ag_sr.at[j], dev(z, xi, 1 - core))

    def hops(first, j):
        along_z = first != (j == last)
        return (ag_z, nz) if along_z else (ag_x, nx)

    order = list(range(chunks)) + [chunks]
    for j in order:
        fn, n = hops(True, j)
        for i in range(1, n):
            fn(j, i).start()

    fwd = pick((grp * ROWS, grp * ROWS), toks, False)
    per_q = grp * toks

    def arrange(ref, width):
        whole = ref[...].reshape(ndev * ROWS, width)
        got = []
        for g in range(ngrp):
            got.append(jnp.dot(fwd, whole[g * grp * ROWS:(g + 1) * grp * ROWS], preferred_element_type=F32))
        return [jnp.concatenate([p[q * per_q:(q + 1) * per_q] for p in got], axis=0) for q in range(quarters)]

    def gate_up(j):
        for c in load_w(j):
            c.wait()
        rows = pl.ds(starts[j], widths[j])
        xc = jnp.concatenate([p.astype(BF16) for p in arrange(x[j], widths[j])], axis=1)
        for acc, wt in ((acc_g, wg), (acc_u, wu)):
            d = jnp.dot(xc, wt[:, rows, :].reshape(quarters * widths[j], hid), preferred_element_type=F32)
            acc[...] = d if j == 0 else acc[...] + d

    for j in [last] + [j for j in order if j != last]:
        fn, n = hops(True, j)
        for i in range(1, n):
            fn(j, i, True).wait_recv()
        fn, n = hops(False, j)
        for i in range(1, n):
            fn(j, i).start()
    for j in order:
        fn, n = hops(False, j)
        for i in range(1, n):
            fn(j, i, True).wait_recv()
        ag_s(j).start()
    for j in order:
        ag_s(j, True).wait_recv()
        if j < chunks:
            gate_up(j)

    own = lax.broadcasted_iota(jnp.int32, (ndev * toks, 128), 1) == z
    aa = functools.reduce(lambda p, q: p + q, arrange(xa, 128)[:3])
    share = jnp.sum(jnp.where(own, aa, 0.0), axis=1, keepdims=True)
    g = acc_g[...]
    h = (g / (1.0 + jnp.exp(-g)) * acc_u[...]).astype(BF16)
    back = pick((grp * ROWS, grp * ROWS), toks, True)

    def rs_s(j):
        return remote(y[j].at[1 - core], r_sib[j], rs_ss.at[j], rs_sr.at[j], dev(z, xi, 1 - core))

    def rs_x(j, i):
        to = lax.rem(xi + i, nx)
        src = s2[j].at[to] if j == last else s1[j].at[to]
        return remote(src, r_x[j].at[i], rs_xs.at[j, i], rs_xr.at[j, i], dev(z, to, core))

    def rs_z(j, i):
        to = lax.rem(z + i, nz)
        src = s1[j].at[:, to] if j == last else s2[j].at[to]
        return remote(src, r_z[j].at[i], rs_zs.at[j, i], rs_zr.at[j, i], dev(to, xi, core))

    for q in range(quarters):
        load_d(q).wait()

    def down(j):
        terms = []
        for q in range(quarters):
            d = jnp.dot(h, wd[:, lanes(q, j)], preferred_element_type=F32)
            terms.append((d * share).astype(BF16))
        out = []
        for gi in range(ngrp):
            rows = jnp.concatenate([v[gi * per_q:(gi + 1) * per_q] for v in terms], axis=0)
            out.append(jnp.dot(back, rows, preferred_element_type=F32).astype(BF16))
        y[j][...] = jnp.concatenate(out, axis=0).reshape(2, nx, nz, ROWS, widths[j])
        rs_s(j).start()

    def first_hop(j):
        rs_s(j).wait_recv()
        s1[j][...] = (y[j][core].astype(F32) + r_sib[j][...].astype(F32)).astype(BF16)
        fn, n = (rs_z, nz) if j == last else (rs_x, nx)
        for i in range(1, n):
            fn(j, i).start()

    def second_hop(j):
        if j == last:
            v = s1[j][:, z].astype(F32)
            for i in range(1, nz):
                rs_z(j, i).wait_recv()
                v = v + r_z[j][i].astype(F32)
        else:
            v = s1[j][xi].astype(F32)
            for i in range(1, nx):
                rs_x(j, i).wait_recv()
                v = v + r_x[j][i].astype(F32)
        s2[j][...] = v.astype(BF16)
        fn, n = (rs_x, nx) if j == last else (rs_z, nz)
        for i in range(1, n):
            fn(j, i).start()

    def stage_out(j):
        if j == last:
            v = s2[j][xi].astype(F32)
            for i in range(1, nx):
                rs_x(j, i).wait_recv()
                v = v + r_x[j][i].astype(F32)
        else:
            v = s2[j][z].astype(F32)
            for i in range(1, nz):
                rs_z(j, i).wait_recv()
                v = v + r_z[j][i].astype(F32)
        for q in range(quarters):
            out_ref[:, lanes(q, j)] = v[q * toks:(q + 1) * toks].astype(BF16)

    turns = [last] + list(range(last))
    for fn in (down, first_hop):
        for j in turns:
            fn(j)
    for fn in (second_hop, stage_out):
        for j in turns[::-1] if fn is second_hop else turns:
            fn(j)

    for j in order:
        for i in range(1, nz):
            ag_z(j, i).wait_send()
        for i in range(1, nx):
            ag_x(j, i).wait_send()
        ag_s(j).wait_send()
    for j in range(chunks):
        for i in range(1, nz):
            rs_z(j, i).wait_send()
        for i in range(1, nx):
            rs_x(j, i).wait_send()
        rs_s(j).wait_send()


def chunk_widths(quarter):
    n = quarter // 128
    small = max(1, (n * 6) // 14)
    return ((n - small) * 128, small * 128)


def on_device(tokens, route, gates, w_gate, w_up, w_down):
    nz = lax.axis_size("ex")
    nx = lax.axis_size("ey") // 2
    toks, width = tokens.shape
    quarters = ROWS // toks
    quarter = width // quarters
    hid = w_gate.shape[2]
    widths = chunk_widths(quarter)
    chunks = len(widths)
    last = chunks - 1
    ndev = 2 * nx * nz
    cfg = (nz, nx, widths, toks, quarters)
    dma = pltpu.SemaphoreType.DMA

    def per_chunk(lead):
        return [pltpu.VMEM(lead(j) + (ROWS, widths[j]), BF16) for j in range(chunks)]

    vm = pl.BlockSpec(memory_space=pltpu.VMEM)
    hbm = pl.BlockSpec(memory_space=pl.ANY)
    return pl.pallas_call(
        functools.partial(kernel, cfg),
        out_shape=jax.ShapeDtypeStruct((toks, width), BF16),
        in_specs=[vm, vm, vm, hbm, hbm, hbm],
        out_specs=vm,
        scratch_shapes=[
            pltpu.VMEM((quarters, quarter, hid), BF16),
            pltpu.VMEM((quarters, quarter, hid), BF16),
            pltpu.VMEM((hid, width), BF16),
            per_chunk(lambda j: (2, nx, nz)),
            pltpu.VMEM((2, nx, nz, ROWS, 128), BF16),
            pltpu.VMEM((ndev * toks, hid), F32),
            pltpu.VMEM((ndev * toks, hid), F32),
            per_chunk(lambda j: (2, nx, nz)),
            per_chunk(lambda j: (nx, nz)),
            per_chunk(lambda j: (nx, nz)),
            per_chunk(lambda j: (nx,) if j == last else (nx, nz)),
            per_chunk(lambda j: (nx,) if j == last else (nz,)),
            per_chunk(lambda j: (nz, nx) if j == last else (nz,)),
            dma((3, max(chunks, quarters))),
            dma((chunks + 1, nz)), dma((chunks + 1, nz)),
            dma((chunks + 1, nx)), dma((chunks + 1, nx)),
            dma((chunks + 1,)), dma((chunks + 1,)),
            dma((chunks, nz)), dma((chunks, nz)),
            dma((chunks, nx)), dma((chunks, nx)),
            dma((chunks,)), dma((chunks,)),
        ],
        compiler_params=pltpu.CompilerParams(
            collective_id=0, has_side_effects=True, vmem_limit_bytes=56 * 1024 * 1024
        ),
    )(tokens, route.T, gates.T, w_gate.reshape(quarters, quarter, hid),
      w_up.reshape(quarters, quarter, hid), w_down[0])


def solution(mesh):
    placed = (
        P(("groups", "ex", "ey"), None),
        P(("groups", "ex", "ey"), None),
        P(("groups", "ex", "ey"), None),
        P("ex", None, "ey"),
        P("ex", None, "ey"),
        P("ex", "ey", None),
    )
    return jax.shard_map(
        on_device,
        mesh=mesh,
        in_specs=placed,
        out_specs=P(("groups", "ex", "ey"), None),
        check_vma=False,
    )
```
